32 devices in a mesh: dm: 4 (over y, x), freq: 8 (over z, core).
Axes of the slice: x: 2, y: 2, z: 4, core: 2. Of those that a mesh axis runs over, the one named last changes fastest.
Arguments:
- series: float32 [16777216], P(('dm', 'freq')), parts along dimension 0, may hold values from -6 to 6
- kernels: float32 [2, 16, 129], replicated, may hold values from -0.5 to 0.5
- half_widths: int32 [16], replicated, may hold values from 32 to 64, as said below
- sub_rows: int32 [3, 16], replicated, may hold values from 0 to 15
Outputs:
- summed: float32 [16, 8388608], P(None, ('dm', 'freq')), parts along dimension 1
The draws below stay inside these ranges and needn't reach their ends.
There are 4 independent parts, one for each index of `dm`. The reference program is written for one: setup_inputs(seed, part) draws one part's arguments, and reference() takes and returns one part's arrays. A program takes and returns all parts, laid end to end along the dimension named above; an argument that names none is the same for every part. Nothing has to cross between parts.
Inputs may be any that keep to these rules, and one draw needn't show every extreme that they name: Template t's kernel is nonzero only at offsets |j| <= half_widths[t]; some template has half-width exactly 64.
All inputs are finite; a program needn't handle non-finite values.
Results may differ from the reference program's by a relative error of at most 0.000051.
Values sent between devices are 32-bit elements; how exact they have to be, the bound alone decides.
A program may use at most 832 MiB of HBM per device.

```python
import math
import jax
import jax.numpy as jnp
from jax import lax

SAMPLES = 4194304
TEMPL = 16
MAXHALF = 64


def draw_half_widths(key, part):
    widths = jax.random.randint(jax.random.fold_in(key, 11), (TEMPL,), MAXHALF // 2, MAXHALF + 1, dtype=jnp.int32)
    chosen = jax.random.randint(jax.random.fold_in(key, 12), (), 0, TEMPL, dtype=jnp.int32)
    return jnp.where(jnp.arange(TEMPL, dtype=jnp.int32) == chosen, MAXHALF, widths).astype(jnp.int32)


def plant(array, own_key, least, largest):
    shape = array.shape
    index_at = [jax.random.randint(jax.random.fold_in(own_key, axis), (), 0, shape[axis]) for axis in range(len(shape))]
    array = array.at[tuple(index_at)].set(least)
    longest = shape.index(max(shape))
    index_at[longest] = (index_at[longest] + 1) % shape[longest]
    return array.at[tuple(index_at)].set(largest)


def shard_levels(own_key, dims, split, smallest, largest):
    loudness, own = 1.0, jax.random.fold_in(own_key, 6)
    for axis_at, shards_of in split:
        heights = jnp.exp(jax.random.uniform(jax.random.fold_in(own, axis_at), (shards_of,), jnp.float32, smallest / len(split), largest / len(split)))
        loudness = loudness * jnp.repeat(heights, dims[axis_at] // shards_of).reshape([-1 if axis == axis_at else 1 for axis in range(len(dims))])
    return loudness


def gaussian(stream_key, dims, scale, most, split=(), held_as=jnp.bfloat16):
    level = shard_levels(stream_key, dims, split, -0.22, 0.18) if split else 1.0
    result = jax.random.normal(stream_key, dims, jnp.float32) * scale * level
    return jnp.minimum(jnp.maximum(result, -most), most).astype(held_as)


def setup_inputs(seed: int = 0, part: int = 0) -> dict:
    arg_keys = jax.random.split(jax.random.key(seed), 5)
    part_keys = jax.random.split(jax.random.fold_in(arg_keys[4], part), 5)
    series = gaussian(part_keys[0], (SAMPLES,), 1.0, 6.0, ((0, 8),), jnp.float32)
    kernels = gaussian(arg_keys[1], (2, TEMPL, 2 * MAXHALF + 1), (2 * MAXHALF + 1) ** -0.5, 0.5, (), jnp.float32)
    half_widths = draw_half_widths(jax.random.fold_in(arg_keys[4], 71), part)
    sub_rows = plant(jax.random.randint(arg_keys[3], (3, TEMPL), 0, TEMPL), jax.random.fold_in(arg_keys[3], 1), 0, TEMPL - 1).astype(jnp.int32)
    return dict(series=series, kernels=kernels, half_widths=half_widths, sub_rows=sub_rows)


def masked_taps(kernels, half_widths):
    tap_count = kernels.shape[2]
    half_span = tap_count // 2
    offsets = jnp.abs(jnp.arange(tap_count, dtype=jnp.int32) - half_span)
    inside = offsets[None, :] <= half_widths[:, None]
    return jnp.where(inside[None, :, :], kernels, jnp.zeros_like(kernels))

def reference(series, kernels, half_widths, sub_rows):
    bin_count = SAMPLES // 2
    half_span = MAXHALF
    spectrum = jnp.fft.rfft(series)[:bin_count] / math.sqrt(SAMPLES)
    padded = jnp.concatenate([spectrum, jnp.zeros_like(spectrum)])
    spread = jnp.fft.fft(padded)
    taps = masked_taps(kernels, half_widths)
    filler = jnp.zeros((2 * bin_count - 2 * half_span - 1,), kernels.dtype)

    def one_template(kernel_pair):
        real_taps, imag_taps = kernel_pair
        front_taps = lax.complex(real_taps[half_span::-1], imag_taps[half_span::-1])
        back_taps = lax.complex(real_taps[2 * half_span:half_span:-1], imag_taps[2 * half_span:half_span:-1])
        kernel = jnp.concatenate([front_taps, lax.complex(filler, filler), back_taps])
        response = jnp.fft.ifft(spread * jnp.fft.fft(kernel))[:bin_count]
        return jnp.real(response) * jnp.real(response) + jnp.imag(response) * jnp.imag(response)
    plane = lax.map(one_template, (taps[0], taps[1]))
    positions = jnp.arange(bin_count, dtype=jnp.int32)
    summed = plane
    for harmonic in range(1, 4):
        row_picks = jnp.take(plane, sub_rows[harmonic - 1], axis=0)
        summed = summed + jnp.take(row_picks, harmonic * positions // 4, axis=1)
    return summed
```

```python
import functools
import math

import jax
import jax.numpy as jnp
import numpy as np
from jax import lax
from jax.experimental import pallas as pl
from jax.experimental.pallas import tpu as pltpu
from jax.sharding import PartitionSpec as P

FACTOR = 2048
LANES = 128
GROUP = 8


highest = lax.Precision.HIGH


def unit_table(left_ints, right_ints, length):
    product = left_ints * right_ints % length
    angles = product.astype(jnp.float32) * (-2.0 * math.pi / length)
    return (jnp.cos(angles), jnp.sin(angles))


def complex_times(left_pair, right_pair):
    return (
        left_pair[0] * right_pair[0] - left_pair[1] * right_pair[1],
        left_pair[0] * right_pair[1] + left_pair[1] * right_pair[0],
    )


def complex_einsum(pattern, left_pair, right_pair):

    def single(one_side, other_side):
        return jnp.einsum(pattern, one_side, other_side, precision=highest)

    return (
        single(left_pair[0], right_pair[0]) - single(left_pair[1], right_pair[1]),
        single(left_pair[0], right_pair[1]) + single(left_pair[1], right_pair[0]),
    )


def forward_spectrum(series, members, position):
    samples = members * series.shape[0]
    rows_lo = FACTOR // members
    cols_lo = series.shape[0] // rows_lo // members
    blocks = series.reshape(rows_lo, members, cols_lo)
    sendable = jnp.transpose(blocks, (1, 0, 2)).reshape(members, rows_lo * cols_lo)
    arrived = lax.all_to_all(sendable, "freq", split_axis=0, concat_axis=0, tiled=True).reshape(
        members, rows_lo, cols_lo
    )
    outer_ids = jnp.arange(members, dtype=jnp.int32)
    inner_ids = jnp.arange(rows_lo, dtype=jnp.int32)
    outer_table = unit_table(outer_ids[:, None], outer_ids[None, :], members)
    first_real = jnp.einsum("pr,rsc->psc", outer_table[0], arrived, precision=highest)
    first_imag = jnp.einsum("pr,rsc->psc", outer_table[1], arrived, precision=highest)
    turned = complex_times(
        (first_real, first_imag),
        unit_table(outer_ids[:, None, None], inner_ids[None, :, None], FACTOR),
    )
    inner_table = unit_table(inner_ids[:, None], inner_ids[None, :], rows_lo)
    columns = complex_einsum("qs,psc->cqp", inner_table, turned)
    column_ids = jnp.arange(cols_lo, dtype=jnp.int32) + position * cols_lo
    frequency_ids = jnp.arange(FACTOR, dtype=jnp.int32)
    columns = complex_times(
        (columns[0].reshape(cols_lo, FACTOR), columns[1].reshape(cols_lo, FACTOR)),
        unit_table(column_ids[:, None], frequency_ids[None, :], samples),
    )

    def arrange(values):
        return jnp.transpose(values.reshape(cols_lo, members, rows_lo), (1, 2, 0)).reshape(
            members, rows_lo * cols_lo
        )

    arrived = (
        lax.all_to_all(arrange(columns[0]), "freq", split_axis=0, concat_axis=0, tiled=True),
        lax.all_to_all(arrange(columns[1]), "freq", split_axis=0, concat_axis=0, tiled=True),
    )
    cube = (
        arrived[0].reshape(members, rows_lo, cols_lo),
        arrived[1].reshape(members, rows_lo, cols_lo),
    )
    second = complex_einsum("pr,ras->pas", outer_table, cube)
    lane_ids = jnp.arange(cols_lo, dtype=jnp.int32)
    turned = complex_times(
        second, unit_table(outer_ids[:, None, None], lane_ids[None, None, :], members * cols_lo)
    )
    row_block = cols_lo // 2
    last_table = unit_table(
        jnp.arange(row_block, dtype=jnp.int32)[:, None], lane_ids[None, :], cols_lo
    )
    spectrum = complex_einsum("qs,pas->qpa", last_table, turned)
    norming = 1.0 / math.sqrt(samples)
    rows_pair = (
        (spectrum[0] * norming).reshape(row_block * members, rows_lo),
        (spectrum[1] * norming).reshape(row_block * members, rows_lo),
    )
    return (rows_pair, row_block, rows_lo)


def toeplitz(kernels, half_widths):
    tap_count = kernels.shape[2]
    half_span = tap_count // 2
    stride = 2 * half_span
    offsets = jnp.abs(jnp.arange(tap_count, dtype=jnp.int32) - half_span)
    inside = offsets[None, :] <= half_widths[:, None]
    masked = jnp.where(inside[None, :, :], kernels, jnp.zeros_like(kernels))
    length = stride + tap_count
    padded = jnp.pad(masked, ((0, 0), (0, 0), (0, stride)))
    repeated = jnp.tile(padded, (1, 1, stride))[:, :, : stride * (length - 1)]
    return repeated.reshape(2, kernels.shape[1], stride, length - 1)


def split_halves(values):
    rounded = lax.reduce_precision(values, exponent_bits=8, mantissa_bits=7)
    return rounded.astype(jnp.bfloat16), (values - rounded).astype(jnp.bfloat16)


def reach(harmonic, half_span):
    return harmonic * LANES // 4 + 2 * half_span


def padded_depth(harmonic, half_span):
    return -(-2 * reach(harmonic, half_span) // LANES) * LANES


def weights(matrices, harmonic, half_span):
    width = reach(harmonic, half_span)
    picks = np.arange(LANES) * harmonic // 4
    chosen = jnp.asarray(np.arange(LANES)[:, None] == picks[None, :], jnp.bfloat16)
    result = []
    for half in split_halves(matrices):
        turned = jnp.einsum(
            "ctmi,ml->ctil", half[..., :width], chosen, preferred_element_type=jnp.float32
        ).astype(jnp.bfloat16)
        real, imag = turned[0], turned[1]
        upper = jnp.concatenate([real, imag], axis=2)
        lower = jnp.concatenate([-imag, real], axis=2)
        both = jnp.concatenate([upper, lower], axis=1)
        extra = padded_depth(harmonic, half_span) - 2 * width
        result.append(jnp.pad(both, ((0, 0), (0, extra), (0, 0))))
    return result


def windows(stretch, harmonic, half_span, blocks):
    step = harmonic * LANES // 4
    width = reach(harmonic, half_span)
    count = -(-width // step)
    short = max(0, (blocks + count - 1) * step - stretch.shape[1])
    stretch = jnp.pad(stretch, ((0, 0), (0, short)))
    pieces = []
    for part in range(2):
        for piece in range(count):
            taken = stretch[part, piece * step : (piece + blocks) * step].reshape(blocks, step)
            pieces.append(taken[:, : min(step, width - piece * step)])
    extra = padded_depth(harmonic, half_span) - 2 * width
    if extra:
        pieces.append(jnp.zeros((blocks, extra), stretch.dtype))
    return jnp.concatenate(pieces, axis=1)


def power_kernel(count, has_base, *refs):
    window_refs = refs[:count]
    weight_refs = refs[count : 3 * count]
    base_ref = refs[3 * count] if has_base else None
    out_ref = refs[3 * count + has_base]
    high_refs = refs[3 * count + has_base + 1 : -1][:count]
    low_refs = refs[3 * count + has_base + 1 : -1][count:]
    held = refs[-1]
    rows = window_refs[0].shape[0]
    for index in range(count):
        values = window_refs[index][...]
        rounded = values.astype(jnp.bfloat16)
        high_refs[index][...] = rounded
        low_refs[index][...] = (values - rounded.astype(jnp.float32)).astype(jnp.bfloat16)
    for template in range(GROUP):
        total = None
        for index in range(count):
            high = weight_refs[2 * index][template]
            low = weight_refs[2 * index + 1][template]
            left = high_refs[index][...]

            def product(one, other):
                return jnp.dot(one, other, preferred_element_type=jnp.float32)

            response = product(left, high) + (
                product(low_refs[index][...], high) + product(left, low)
            )
            real, imag = response[:, :LANES], response[:, LANES:]
            power = real * real + imag * imag
            total = power if total is None else total + power
        held[pl.ds(template, rows, stride=GROUP), :] = total
    for row in range(rows):
        values = held[row * GROUP : (row + 1) * GROUP, :]
        place = slice(row * LANES, (row + 1) * LANES)
        if has_base:
            values = values + base_ref[:, place]
        out_ref[:, place] = values


def powers(window_list, weight_list, base):
    count = len(window_list)
    blocks = window_list[0].shape[0]
    templates = weight_list[0].shape[0]
    rows = min(256, blocks)
    depths = [window.shape[1] for window in window_list]
    in_specs = [pl.BlockSpec((rows, depth), lambda t, m: (m, 0)) for depth in depths]
    in_specs += [
        pl.BlockSpec((GROUP, weight.shape[1], 2 * LANES), lambda t, m: (t, 0, 0))
        for weight in weight_list
    ]
    out_spec = pl.BlockSpec((GROUP, rows * LANES), lambda t, m: (t, m))
    operands = [*window_list, *weight_list]
    aliases = {}
    if base is not None:
        in_specs.append(out_spec)
        aliases = {len(operands): 0}
        operands.append(base)
    flops = 2 * 3 * blocks * sum(depths) * templates * 2 * LANES
    return pl.pallas_call(
        functools.partial(power_kernel, count, int(base is not None)),
        out_shape=jax.ShapeDtypeStruct((templates, blocks * LANES), jnp.float32),
        grid=(templates // GROUP, blocks // rows),
        in_specs=in_specs,
        out_specs=out_spec,
        scratch_shapes=[pltpu.VMEM((rows, depth), jnp.bfloat16) for depth in depths] * 2
        + [pltpu.VMEM((rows * GROUP, LANES), jnp.float32)],
        input_output_aliases=aliases,
        compiler_params=pltpu.CompilerParams(vmem_limit_bytes=58 * 1024 * 1024),
        cost_estimate=pl.CostEstimate(
            flops=flops,
            bytes_accessed=4 * blocks * (2 * sum(depths) + templates * LANES),
            transcendentals=0,
        ),
    )(*operands)


def fetched(rows_pair, members, ranges):
    freq_rows = rows_pair[0].shape[1]
    both = jnp.stack([jnp.pad(rows, ((1, 1), (0, 0))) for rows in rows_pair])
    total = sum(count + 2 for _, count in ranges)
    extra = -total % 8
    slabs = []
    for target in range(members):
        pieces = [both[:, target * count : target * count + count + 2] for _, count in ranges]
        pieces.append(jnp.zeros((2, extra, freq_rows), both.dtype))
        slabs.append(jnp.concatenate(pieces, axis=1))
    arrived = lax.all_to_all(jnp.stack(slabs), "freq", split_axis=0, concat_axis=0, tiled=True)
    lined = jnp.transpose(arrived, (1, 2, 0, 3)).reshape(2, total + extra, members * freq_rows)
    result = []
    first = 0
    for _, count in ranges:
        result.append(
            lined[:, first : first + count + 2].reshape(2, (count + 2) * members * freq_rows)
        )
        first += count + 2
    return result


def on_device(series, kernels, half_widths, sub_rows):
    members = lax.axis_size("freq")
    position = lax.axis_index("freq")
    rows_pair, row_block, freq_rows = forward_spectrum(series, members, position)
    half_span = kernels.shape[2] // 2
    blocks = row_block * FACTOR // LANES
    matrices = toeplitz(kernels, half_widths)

    def cut(stretch):
        return stretch[:, FACTOR - half_span :]

    own = fetched(rows_pair, members, [(4, row_block)])
    lower = fetched(rows_pair, members, [(h, h * row_block // 4) for h in range(1, 4)])
    plane = powers(
        [windows(cut(own[0]), 4, half_span, blocks)], weights(matrices, 4, half_span), None
    )
    window_list, weight_list = [], []
    for harmonic in range(1, 4):
        window_list.append(windows(cut(lower[harmonic - 1]), harmonic, half_span, blocks))
        chosen = jnp.take(matrices, sub_rows[harmonic - 1], axis=1)
        weight_list.extend(weights(chosen, harmonic, half_span))
    return powers(window_list, weight_list, plane)


def solution(mesh):
    in_specs = (P(("dm", "freq")), P(), P(), P())
    out_specs = P(None, ("dm", "freq"))
    return jax.shard_map(
        on_device, mesh=mesh, in_specs=in_specs, out_specs=out_specs, check_vma=False
    )
```
